32 devices in a mesh: section: 2 (over core), batch: 16 (over z, y, x).
Axes of the slice: x: 2, y: 2, z: 4, core: 2. Of those that a mesh axis runs over, the one named last changes fastest.
Arguments:
- inputs: bfloat16 [2, 32, 256, 512], P('section', 'batch'), may hold values from -6 to 6
- cotangent: bfloat16 [2, 32, 256, 512], P('section', 'batch'), may hold values from -6 to 6
- lengths: int32 [32, 2, 4], P('batch'), may hold values from 1 to 96, 256 in all within a row
- norm_gain: float32 [2, 3, 512], P('section'), may hold values from 0.5 to 1.5
- norm_bias: float32 [2, 3, 512], P('section'), may hold values from -1.5 to 1.5
- attn_qkv: bfloat16 [2, 512, 1536], P('section'), may hold values from -0.25 to 0.25
- attn_out: bfloat16 [2, 512, 512], P('section'), may hold values from -1.5 to 1.5
- ffn_in: bfloat16 [2, 512, 2048], P('section'), may hold values from -0.25 to 0.25
- ffn_out: bfloat16 [2, 2048, 512], P('section'), may hold values from -0.125 to 0.125
- cross_proj: bfloat16 [2, 512, 1024], P('section'), may hold values from -0.75130096 to 0.75130096
Outputs:
- outputs: bfloat16 [2, 32, 256, 512], P('section', 'batch')
- input_grads: float32 [2, 32, 256, 512], P('section', 'batch')
- gain_grads: float32 [2, 3, 512], P('section', None, 'batch')
- bias_grads: float32 [2, 3, 512], P('section', None, 'batch')
- qkv_grads: float32 [2, 512, 1536], P('section', 'batch')
- out_grads: float32 [2, 512, 512], P('section', 'batch')
- in_grads: float32 [2, 512, 2048], P('section', 'batch')
- down_grads: float32 [2, 2048, 512], P('section', 'batch')
- cross_grads: float32 [2, 512, 1024], P('section', 'batch')
The draws below stay inside these ranges and needn't reach their ends.
Inputs may be any that keep to these rules, and one draw needn't show every extreme that they name: Both rows of an index hold 4 molecules each, molecule s of the decoder row paired with molecule s of the encoder row; each row's lengths sum to 256.
All inputs are finite; a program needn't handle non-finite values.
Results may differ from the reference program's by a relative error of at most 0.014.
Values may be sent and summed in bfloat16 or wider, within the bound.
No kernel may reach another device: no remote copies, remote signals or barrier semaphores. Data moves between devices by JAX's collectives and lax.ppermute only.
A program may use at most 256 MiB of HBM per device.

```python
import math
import jax
import jax.numpy as jnp
import numpy as np
from jax import lax

D = 512
HEADS = 8
HEAD_DIM = 64
FF = 2048
SEQ = 256
SEGS = 4
MOST = 96
ROWS = 32


def draw_cross_proj(key, part):
    key = jax.random.fold_in(key, 7)
    values = jax.random.truncated_normal(key, -3.0, 3.0, (2, D, 2 * D), jnp.float32)
    blocks = jnp.arange(2)[:, None, None]
    columns = jnp.arange(2 * D)[None, None, :]
    widened = (blocks == 1) & (columns >= D)
    factor = jnp.where(widened, 32.0 ** 0.5, 1.0) * D ** (-0.5)
    return (values * factor).astype(jnp.bfloat16)


def spiked(result, stream_key, source, target, shards_of, factor):
    def block_of(position):
        return (jnp.arange(result.shape[position]) // (result.shape[position] // shards_of)).reshape((-1,) + (1,) * (result.ndim - 1 - position))

    near = jax.random.permutation(stream_key, shards_of)[block_of(target)]
    second = (block_of(target) + shards_of // 2) % shards_of
    return jnp.where((block_of(source) == near) | (block_of(source) == second), factor * result, result)


def level_of(rng, dims, shards, smallest, top_value):
    level, own = 1.0, jax.random.fold_in(rng, 6)
    for axis_at, shards_of in shards:
        heights = jnp.exp(jax.random.uniform(jax.random.fold_in(own, axis_at), (shards_of,), jnp.float32, smallest / len(shards), top_value / len(shards)))
        level = level * jnp.repeat(heights, dims[axis_at] // shards_of).reshape([-1 if axis == axis_at else 1 for axis in range(len(dims))])
    return level


def profile(amount, total, most, slope):
    weights = [(1 << 20) // math.isqrt(standing ** slope) + 1 for standing in range(2, amount + 1)]
    rest, counts = total - most - (amount - 1), [1] * (amount - 1)
    while rest > 0:
        movable = [i for i in range(amount - 1) if counts[i] < most]
        mass, remaining = sum([weights[i] for i in movable]), rest
        for i in movable:
            addition = min(most - counts[i], max(1, remaining * weights[i] // mass), rest)
            counts[i] = counts[i] + addition
            rest = rest - addition
    return np.array([most] + counts)


def uneven_parts(key, amount, total, reach, lean):
    if amount == 2:
        one = jax.random.randint(key, (), max(1, total - reach), min(reach, total - 1) + 1)
        return jnp.stack([one, total - one])
    sizes = jnp.asarray(profile(amount, total, reach, lean), jnp.int32)
    pairs = (amount - 1) // 2
    giver, taker = sizes[1:1 + 2 * pairs:2], sizes[2:2 + 2 * pairs:2]
    margin = jnp.minimum(giver - 1, reach - taker)
    shifted = jax.random.randint(jax.random.fold_in(key, 1), (pairs,), 0, 1 << 20) % (margin + 1)
    sizes = sizes.at[1:1 + 2 * pairs:2].set(giver - shifted).at[2:2 + 2 * pairs:2].set(taker + shifted)
    return sizes[jax.random.permutation(jax.random.fold_in(key, 2), amount)]


def noise(key, shape, scale, reach, shards=(), kind=jnp.bfloat16):
    level = level_of(key, shape, shards, -0.22, 0.18) if shards else 1.0
    entries = jax.random.normal(key, shape, jnp.float32) * scale * level
    return jnp.minimum(jnp.maximum(entries, -reach), reach).astype(kind)


def noise_with(rng, shape, width, reach, cuts, heavy, kind=jnp.bfloat16):
    array = width * jax.random.normal(rng, shape, jnp.float32)
    if cuts:
        array = array * level_of(rng, shape, cuts, -0.22, 0.18)
    return jnp.clip(spiked(array, jax.random.fold_in(rng, 3), *heavy), -reach, reach).astype(kind)


def setup_inputs(seed: int = 0) -> dict:
    arg_keys = jax.random.split(jax.random.key(seed), 11)
    inputs = noise_with(arg_keys[0], (2, ROWS, SEQ, D), 1.0, 6.0, ((0, 2), (1, 16)), (1, 3, 16, 2.0))
    cotangent = noise(arg_keys[1], (2, ROWS, SEQ, D), 1.0, 6.0, ((0, 2), (1, 16)))
    lengths = jax.vmap(lambda own: uneven_parts(own, SEGS, SEQ, MOST, 2))(jax.random.split(arg_keys[2], ROWS * 2)).reshape((ROWS, 2, SEGS)).astype(jnp.int32)
    norm_gain = jnp.clip(1.0 + 0.1 * jax.random.normal(arg_keys[3], (2, 3, D), jnp.float32), 0.5, 1.5)
    norm_bias = noise(arg_keys[4], (2, 3, D), 0.3, 1.5, ((0, 2),), jnp.float32)
    attn_qkv = noise(arg_keys[5], (2, D, 3 * D), D ** -0.5, 0.25, ((0, 2),))
    attn_out = noise(arg_keys[6], (2, D, D), (D // 32) ** -0.5, 1.5, ((0, 2),))
    ffn_in = noise(arg_keys[7], (2, D, FF), D ** -0.5, 0.25, ((0, 2),))
    ffn_out = noise(arg_keys[8], (2, FF, D), FF ** -0.5, 0.125, ((0, 2),))
    cross_proj = draw_cross_proj(jax.random.fold_in(arg_keys[10], 71), 0)
    return {"inputs": inputs, "cotangent": cotangent, "lengths": lengths, "norm_gain": norm_gain, "norm_bias": norm_bias, "attn_qkv": attn_qkv, "attn_out": attn_out, "ffn_in": ffn_in, "ffn_out": ffn_out, "cross_proj": cross_proj}


@jax.custom_vjp
def low(v):
    return lax.optimization_barrier(v.astype(jnp.bfloat16)).astype(jnp.float32)

@jax.custom_vjp
def low_back(v):
    return v

def low_keep(v):
    return (low(v), None)

def low_pass(kept, grad):
    return (grad,)

def back_keep(v):
    return (v, None)

def back_low(kept, grad):
    return (low(grad),)
low.defvjp(low_keep, low_pass)
low_back.defvjp(back_keep, back_low)
epsilon = 1e-05
score_scale = 0.125
masked_score = -1000000000.0

def matmul(left_side, right_side):
    return jnp.dot(left_side, right_side, precision=lax.Precision.HIGHEST)

def layer_norm(values, gain_vec, bias_vec):
    average = lax.optimization_barrier(jnp.mean(values, axis=-1, keepdims=True))
    centered = values - average
    variance = lax.optimization_barrier(jnp.mean(centered * centered, axis=-1, keepdims=True))
    return centered * lax.rsqrt(variance + epsilon) * gain_vec + bias_vec

def attend(queries, key_rows, values, allowed):
    query_count = queries.shape[0]
    query_heads = queries.reshape(query_count, HEADS, HEAD_DIM)
    key_heads = key_rows.reshape(key_rows.shape[0], HEADS, HEAD_DIM)
    value_heads = values.reshape(values.shape[0], HEADS, HEAD_DIM)
    scores = jnp.einsum('qhd,khd->hqk', query_heads, key_heads, precision=lax.Precision.HIGHEST) * score_scale
    scores = low_back(jnp.where(allowed[None], scores, masked_score))
    attn_probs = low(jax.nn.softmax(scores, axis=-1))
    mixed_rows = jnp.einsum('hqk,khd->qhd', attn_probs, value_heads, precision=lax.Precision.HIGHEST)
    return low_back(low(mixed_rows.reshape(query_count, HEADS * HEAD_DIM)))

def self_part(hidden, gain_vec, bias_vec, w_qkv, w_out, allowed):
    normed = low(layer_norm(hidden, gain_vec, bias_vec))
    projected = low_back(low(matmul(normed, w_qkv)))
    mixed_rows = attend(projected[:, :D], projected[:, D:2 * D], projected[:, 2 * D:], allowed)
    return hidden + low_back(matmul(mixed_rows, w_out))

def feed_part(hidden, gain_vec, bias_vec, w_in, w_down):
    normed = low(layer_norm(hidden, gain_vec, bias_vec))
    pre_active = low_back(matmul(normed, w_in))
    active = low(jax.nn.gelu(pre_active, approximate=False))
    return hidden + low_back(matmul(active, w_down))

def one_row(params, row_data):
    gain_rows, biases, w_qkv, w_out, w_in, w_down, w_cross = params
    source_row, target_row, source_ids, target_ids = row_data
    places = jnp.arange(SEQ, dtype=jnp.int32)
    same_source = source_ids[:, None] == source_ids[None, :]
    causal = (target_ids[:, None] == target_ids[None, :]) & (places[None, :] <= places[:, None])
    cross_mask = target_ids[:, None] == source_ids[None, :]
    after_self = self_part(source_row, gain_rows[0, 0], biases[0, 0], w_qkv[0], w_out[0], same_source)
    after_feed = feed_part(after_self, gain_rows[0, 1], biases[0, 1], w_in[0], w_down[0])
    memory = low(layer_norm(after_feed, gain_rows[0, 2], biases[0, 2]))
    keys_values = low_back(low(matmul(memory, w_cross[0])))
    upper = self_part(target_row, gain_rows[1, 0], biases[1, 0], w_qkv[1], w_out[1], causal)
    normed = low(layer_norm(upper, gain_rows[1, 1], biases[1, 1]))
    queries = low_back(low(matmul(normed, w_cross[1, :, :D])))
    mixed_rows = attend(queries, keys_values[:, :D], keys_values[:, D:], cross_mask)
    upper = upper + low_back(matmul(mixed_rows, w_cross[1, :, D:]))
    upper = feed_part(upper, gain_rows[1, 2], biases[1, 2], w_in[1], w_down[1])
    return (memory, low(upper))

def reference(inputs, cotangent, lengths, norm_gain, norm_bias, attn_qkv, attn_out, ffn_in, ffn_out, cross_proj):
    segment_ends = jnp.cumsum(lengths, axis=-1)
    places = jnp.arange(SEQ, dtype=jnp.int32)
    segment_ids = lax.optimization_barrier(jnp.sum((segment_ends[..., None, :] <= places[:, None]).astype(jnp.int32), axis=-1))
    source_ids = segment_ids[:, 0]
    target_ids = segment_ids[:, 1]
    checked = jax.checkpoint(one_row)

    def forward(tokens, gain_rows, biases, w_qkv, w_out, w_in, w_down, w_cross):
        params = (gain_rows, biases, w_qkv, w_out, w_in, w_down, w_cross)
        encoded, decoded = lax.map(lambda row_data: checked(params, row_data), (tokens[0], tokens[1], source_ids, target_ids))
        return jnp.stack([encoded, decoded])
    outputs, pullback = jax.vjp(forward, inputs.astype(jnp.float32), norm_gain.astype(jnp.float32), norm_bias.astype(jnp.float32), attn_qkv.astype(jnp.float32), attn_out.astype(jnp.float32), ffn_in.astype(jnp.float32), ffn_out.astype(jnp.float32), cross_proj.astype(jnp.float32))
    grads = pullback(cotangent.astype(jnp.float32))
    return (outputs.astype(jnp.bfloat16), grads[0], grads[1], grads[2], grads[3], grads[4], grads[5], grads[6], grads[7])
```

```python
import math

import jax
import jax.numpy as jnp
from jax import lax
from jax.experimental import pallas as pl
from jax.experimental.pallas import tpu as pltpu
from jax.sharding import PartitionSpec as P

D = 512
HEADS = 8
HEAD_DIM = 64
FF = 2048
SEQ = 256
PAIRS = 4
LANES = 128
CHUNK = 128
TILE = 512
VMEM_LIMIT = 63 * 1024 * 1024

epsilon = 1e-05
score_scale = 0.125
log2_e = 1.4426950408889634
masked_score = -1000000000.0
bf16 = jnp.bfloat16
f32 = jnp.float32


def nn(left, right):
    return lax.dot_general(left, right, (((1,), (0,)), ((), ())), preferred_element_type=f32)


def nt(left, right):
    return lax.dot_general(left, right, (((1,), (1,)), ((), ())), preferred_element_type=f32)


def tn(left, right):
    return lax.dot_general(left, right, (((0,), (0,)), ((), ())), preferred_element_type=f32)


def loop(count, step, together=None):
    if together is None or together >= count:
        for i in range(count):
            step(i)
        return

    def run(i, carry):
        for j in range(together):
            step(i * together + j)
        return carry

    lax.fori_loop(0, count // together, run, 0)


def tile_at(i, size):
    at = i * size
    return pl.ds(at if isinstance(at, int) else pl.multiple_of(at, size), size)


def columns_at(base, i):
    at = base + i * LANES
    return pl.ds(at if isinstance(at, int) else pl.multiple_of(at, LANES), LANES)


def standardized(values):
    average = jnp.mean(values, axis=-1, keepdims=True)
    centered = values - average
    variance = jnp.mean(centered * centered, axis=-1, keepdims=True)
    scale = lax.rsqrt(variance + epsilon)
    return centered * scale, scale


def norm_forward(hidden_ref, gain, bias, normed_ref, together=None):
    def step(i):
        rows = tile_at(i, CHUNK)
        hat, scale = standardized(hidden_ref[rows, :].astype(f32))
        normed_ref[rows, :] = (hat * gain + bias).astype(bf16)

    loop(hidden_ref.shape[0] // CHUNK, step, together)


def norm_backward(hidden_ref, gain, bias, grad_ref, carried_ref, out_ref, sums_ref, place, normed_ref=None):
    def step(i, sums):
        rows = tile_at(i, CHUNK)
        hat, scale = standardized(hidden_ref[rows, :].astype(f32))
        if normed_ref is not None:
            normed_ref[rows, :] = (hat * gain + bias).astype(bf16)
        grad = grad_ref[rows, :].astype(f32)
        grad_hat = grad * gain
        first = jnp.mean(grad_hat, axis=-1, keepdims=True)
        second = jnp.mean(grad_hat * hat, axis=-1, keepdims=True)
        result = scale * (grad_hat - first - hat * second)
        if carried_ref is not None:
            result = result + carried_ref[rows, :].astype(f32)
        out_ref[rows, :] = result
        gain_sum = jnp.sum(grad * hat, axis=0, keepdims=True)
        bias_sum = jnp.sum(grad, axis=0, keepdims=True)
        return (sums[0] + gain_sum, sums[1] + bias_sum)

    sums = (jnp.zeros((1, D), f32), jnp.zeros((1, D), f32))
    for i in range(hidden_ref.shape[0] // CHUNK):
        sums = step(i, sums)
    gain_sum, bias_sum = sums
    sums_ref[pl.ds(place, 1), :] = gain_sum
    sums_ref[pl.ds(place + 3, 1), :] = bias_sum


def half_masks():
    lane = lax.broadcasted_iota(jnp.int32, (1, LANES), 1)
    return [(lane < HEAD_DIM).astype(f32), (lane >= HEAD_DIM).astype(f32)]


def pair_of(parts):
    lane = lax.broadcasted_iota(jnp.int32, parts[0].shape, 1)
    return jnp.where(lane < HEAD_DIM, parts[0], parts[1])


def segments(positions, lengths_ref, row, kind):
    end = jnp.int32(0)
    ids = jnp.zeros_like(positions)
    for i in range(4):
        end = end + lengths_ref[row, kind, i]
        ids = ids + (positions >= end).astype(jnp.int32)
    return ids


def mask_bias(lengths_ref, row, key_kind, query_kind, free):
    keys = lax.broadcasted_iota(jnp.int32, (SEQ, SEQ), 0)
    queries = lax.broadcasted_iota(jnp.int32, (SEQ, SEQ), 1)
    key_ids = segments(keys, lengths_ref, row, key_kind)
    query_ids = segments(queries, lengths_ref, row, query_kind)
    allowed = key_ids == query_ids
    if free is not None:
        allowed = allowed & (keys <= queries + free)
    return jnp.where(allowed, 0.0, masked_score).astype(f32)


def attention_forward(q_ref, q_at, k_ref, k_at, v_ref, v_at, bias_ref, probs_ref, mixed_ref, together=None):
    masks = half_masks()

    def step(i):
        row, pair = (divmod(i, PAIRS)) if isinstance(i, int) else (lax.div(i, PAIRS), lax.rem(i, PAIRS))
        rows = tile_at(row, SEQ)
        columns = lambda base: columns_at(base, pair)
        q = q_ref[rows, columns(q_at)]
        k = k_ref[rows, columns(k_at)].astype(f32)
        v = v_ref[rows, columns(v_at)]
        bias = bias_ref[row]
        mixed = []
        for side in range(2):
            scores = nt((k * masks[side]).astype(bf16), q) * (score_scale * log2_e) + bias
            powers = jnp.exp2(scores - jnp.max(scores, axis=0, keepdims=True))
            probs = (powers * (1.0 / jnp.sum(powers, axis=0, keepdims=True))).astype(bf16)
            probs_ref[2 * i + side] = probs
            mixed.append(tn(probs, v))
        mixed_ref[rows, columns(0)] = pair_of(mixed).astype(bf16)

    loop(bias_ref.shape[0] * PAIRS, step, together)


def attention_backward(
    q_ref, q_at, k_ref, k_at, v_ref, v_at, probs_ref, grad_ref, dq_ref, dq_at, dk_ref, dk_at, dv_ref, dv_at,
    together=None, scores_ref=None,
):
    masks = half_masks()

    def step(i):
        row, pair = (divmod(i, PAIRS)) if isinstance(i, int) else (lax.div(i, PAIRS), lax.rem(i, PAIRS))
        rows = tile_at(row, SEQ)
        columns = lambda base: columns_at(base, pair)
        q = q_ref[rows, columns(q_at)]
        k = k_ref[rows, columns(k_at)]
        v = v_ref[rows, columns(v_at)].astype(f32)
        grad = grad_ref[rows, columns(0)]
        dq, dk, dv = [], [], []
        for side in range(2):
            probs = probs_ref[2 * i + side]
            grad_probs = nt((v * masks[side]).astype(bf16), grad)
            wide = probs.astype(f32)
            inner = jnp.sum(wide * grad_probs, axis=0, keepdims=True)
            grad_scores = (wide * (grad_probs - inner)).astype(bf16)
            dv.append(nn(probs, grad))
            dk.append(nn(grad_scores, q))
            if scores_ref is None:
                dq.append(tn(grad_scores, k))
            else:
                scores_ref[2 * i + side] = grad_scores
        if scores_ref is None:
            dq_ref[rows, columns(dq_at)] = (pair_of(dq) * score_scale).astype(bf16)
        dk_ref[rows, columns(dk_at)] = (pair_of(dk) * score_scale).astype(bf16)
        dv_ref[rows, columns(dv_at)] = pair_of(dv).astype(bf16)

    loop(grad_ref.shape[0] // SEQ * PAIRS, step, together)


def query_gradient(scores_ref, k_ref, dq_ref, together=None):
    def step(i):
        row, pair = (divmod(i, PAIRS)) if isinstance(i, int) else (lax.div(i, PAIRS), lax.rem(i, PAIRS))
        rows, columns = tile_at(row, SEQ), columns_at(0, pair)
        k = k_ref[rows, columns]
        dq = [tn(scores_ref[2 * i + side], k) for side in range(2)]
        dq_ref[rows, columns] = (pair_of(dq) * score_scale).astype(bf16)

    loop(dq_ref.shape[0] // SEQ * PAIRS, step, together)


def gelu_pair(v):
    size = jnp.abs(v)
    base = 1.0 + (0.3275911 * 0.7071067811865476) * size
    t = pl.reciprocal(base, approx=True)
    t = t * (2.0 - base * t)
    series = t * (0.127414796 + t * (-0.142248368 + t * (0.7107068705 + t * (-0.7265760135 + t * 0.5307027145))))
    power = jnp.exp2(v * v * (-0.5 * log2_e))
    value = jnp.maximum(v, 0.0) - size * (series * power)
    lower = power * (series - 0.3989422804014327 * size)
    return value, jnp.where(v >= 0.0, 1.0 - lower, lower)


def put_grad(grad_ref, i, value):
    lead = grad_ref.shape[:-2]
    rows = D // math.prod(lead)
    grad_ref[:, :, :, tile_at(i, rows), :] = value.astype(bf16).reshape(lead + (rows, TILE))


def put_turned(grad_ref, i, value, near):
    rows = D // 16
    blocks = value.astype(bf16).reshape(2, 2, 2, 2, rows, TILE)
    for x in range(2):
        for other in range(2):
            if near:
                grad_ref[:, :, x, other, tile_at(i, rows), :] = blocks[:, :, other, x]
            else:
                grad_ref[:, x, :, other, tile_at(i, rows), :] = blocks[:, other, :, x]


def end_kernel(
    qv_keep, k_keep, o_keep, came, sums, place_ref,
    qkv_out, o_out, gain_out, bias_out,
    qkv, o, gains, biases, semaphores,
):
    rows = k_keep.shape[0]
    place = place_ref[0]
    add = lambda kept, start: kept.astype(f32) + came[start : start + rows, :].astype(f32)
    qkv[:, 0:D] = add(qv_keep[0:rows, :], 0)
    qkv[:, 2 * D : 3 * D] = add(qv_keep[rows : 2 * rows, :], rows)
    qkv[:, D : 2 * D] = add(k_keep[...], 2 * rows)
    o[...] = add(o_keep[...], 3 * rows)
    copies = Copies(semaphores)
    saves = [copies.start(qkv, qkv_out), copies.start(o, o_out)]
    width = gains.shape[-1]
    column = lax.broadcasted_iota(jnp.int32, (D, width), 0)
    own = place * width + lax.broadcasted_iota(jnp.int32, (D, width), 1)
    total = sums[...] + came[4 * rows : 4 * rows + 16, :].astype(f32)[0:8]
    picked = lax.dot_general(
        total, (column == own).astype(f32), (((1,), (0,)), ((), ())),
        preferred_element_type=f32, precision=lax.Precision.HIGHEST,
    )
    for i in range(3):
        gains[i] = picked[i : i + 1, :]
        biases[i] = picked[i + 3 : i + 4, :]
    saves += [copies.start(gains, gain_out), copies.start(biases, bias_out)]
    for save in saves:
        save.wait()


def send_rows(copies, piece, place, bit, start, send_out, keep_out):
    mine = lax.rem(lax.div(place, 2**bit), 2)
    started = []
    for target, at in ((send_out, 1 - mine), (keep_out, mine)):
        for far in range(2):
            for other in range(2):
                source = piece(far, at, other)
                rows = source.shape[-2]
                started.append(copies.start(source, target.at[:, far, pl.ds(start + other * rows, rows), :]))
    return started


def send_halves(copies, grad_ref, place, bit, send_out, keep_out):
    if grad_ref.shape[1] == 1:
        return [copies.start(grad_ref, send_out)]
    mine = lax.rem(lax.div(place, 2**bit), 2)
    return [
        copies.start(grad_ref.at[:, 1 - mine], send_out),
        copies.start(grad_ref.at[:, mine], keep_out),
    ]


class Copies:
    def __init__(self, semaphores):
        self.semaphores = semaphores
        self.count = 0

    def same(self, source, target, at):
        return pltpu.make_async_copy(source, target, self.semaphores.at[at])

    def start(self, source, target):
        copy = self.same(source, target, self.count)
        self.count += 1
        copy.start()
        return copy


def forward_kernel(
    section_ref, lengths_ref, tokens_in, gain_in, bias_in,
    qkv_w, out_w, in_w, down_w, cross_w,
    memory_out, kv_out, qkv_out, probs_out, mixed_out, first_out, active_out, slope_out, second_out,
    query_normed_out, queries_out, normed_out,
    w_qkv, w_o, w_in, w_down, w_cross, normed, qkv, probs, mixed, first, active, slope, second, kv, mask,
    tokens_ref, late_normed, queries, gains, biases, semaphores,
):
    section = section_ref[0]
    tokens = tokens_ref.shape[0]
    copies = Copies(semaphores)
    loads = [copies.start(gain_in, gains), copies.start(bias_in, biases), copies.start(tokens_in, tokens_ref)]
    load_qkv = copies.start(qkv_w, w_qkv)
    load_o = copies.start(out_w, w_o)
    load_in = copies.start(in_w, w_in)
    load_down = copies.start(down_w, w_down)
    load_cross = copies.start(cross_w, w_cross)

    free = jnp.where(section == 0, SEQ, 0)
    for row in range(tokens // SEQ):
        mask[row] = mask_bias(lengths_ref, row, section, section, free)
    for load in loads:
        load.wait()
    norm_forward(tokens_ref, gains[0], biases[0], normed)
    load_qkv.wait()

    def project(i):
        columns = tile_at(i, TILE)
        qkv[:, columns] = nn(normed[...], w_qkv[:, columns]).astype(bf16)

    loop(3 * D // TILE, project)
    save_qkv = copies.start(qkv, qkv_out)
    save_normed = copies.start(normed, normed_out)
    attention_forward(qkv, 0, qkv, D, qkv, 2 * D, mask, probs, mixed)
    save_probs = copies.start(probs, probs_out)
    save_mixed = copies.start(mixed, mixed_out)
    load_o.wait()
    first[...] = tokens_ref[...].astype(f32) + nn(mixed[...], w_o[...])
    save_first = copies.start(first, first_out)
    load_in.wait()
    load_down.wait()
    load_cross.wait()

    @pl.when(section == 0)
    def encoder():
        own = Copies(semaphores)
        own.count = copies.count
        norm_forward(first, gains[1], biases[1], late_normed)
        saves = [own.start(late_normed, query_normed_out)]

        def widen(i):
            columns = tile_at(i, TILE)
            value, derivative = gelu_pair(nn(late_normed[...], w_in[:, columns]))
            active[:, columns] = value.astype(bf16)
            slope[:, columns] = derivative.astype(bf16)

        loop(FF // TILE, widen)
        saves += [own.start(active, active_out), own.start(slope, slope_out)]
        second[...] = first[...] + nn(active[...], w_down[...])
        saves.append(own.start(second, second_out))
        norm_forward(second, gains[2], biases[2], queries)
        saves.append(own.start(queries, memory_out))

        def keyed(i):
            columns = tile_at(i, TILE)
            kv[:, columns] = nn(queries[...], w_cross[:, columns]).astype(bf16)

        loop(2 * D // TILE, keyed)
        saves.append(own.start(kv, kv_out))
        for save in saves:
            save.wait()

    @pl.when(section == 1)
    def decoder():
        own = Copies(semaphores)
        own.count = copies.count
        norm_forward(first, gains[1], biases[1], late_normed, together=2)
        saves = [own.start(late_normed, query_normed_out)]
        queries[...] = nn(late_normed[...], w_cross[:, 0:D]).astype(bf16)
        saves.append(own.start(queries, queries_out))
        for save in saves:
            save.wait()

    save_normed.wait()
    save_qkv.wait()
    save_probs.wait()
    save_mixed.wait()
    save_first.wait()


def middle_kernel(
    section_ref, lengths_ref, kv_in, first_in, queries_in, cotangent_in, gain_in, bias_in,
    in_w, down_w, cross_w,
    dkv_out, sums_out,
    scores_out, mixed_out, branch_out, ffn_normed_out, active_out, slope_out, second_out, carried_out,
    w_in, w_down, w_cross, kv, first, cotangent, queries, probs, mixed, second, ffn_normed, active, slope,
    grad, branch, grad_mixed, scores, dkv, mask, carried, gains, biases, semaphores,
):
    section = section_ref[0]

    @pl.when(section == 1)
    def decoder():
        tokens = first.shape[0]
        copies = Copies(semaphores)
        load_queries = copies.start(queries_in, queries)
        load_kv = copies.start(kv_in, kv)
        loads = [copies.start(gain_in, gains), copies.start(bias_in, biases), copies.start(first_in, first)]
        load_cross = copies.start(cross_w, w_cross)
        load_in = copies.start(in_w, w_in)
        load_down = copies.start(down_w, w_down)
        load_cotangent = copies.start(cotangent_in, cotangent)
        for row in range(tokens // SEQ):
            mask[row] = mask_bias(lengths_ref, row, 0, 1, None)
        load_queries.wait()
        load_kv.wait()
        attention_forward(queries, 0, kv, 0, kv, D, mask, probs, mixed, together=4)
        for load in loads:
            load.wait()
        load_cross.wait()
        second[...] = first[...] + nn(mixed[...], w_cross[:, D : 2 * D])
        norm_forward(second, gains[2], biases[2], ffn_normed, together=2)
        load_in.wait()
        load_down.wait()
        load_cotangent.wait()

        def widen(i):
            columns = tile_at(i, TILE)
            value, derivative = gelu_pair(nn(ffn_normed[...], w_in[:, columns]))
            active[:, columns] = value.astype(bf16)
            slope[:, columns] = (derivative * nt(cotangent[...], w_down[columns, :])).astype(bf16)

        loop(FF // TILE, widen, together=2)
        saves = [
            copies.start(mixed, mixed_out),
            copies.start(ffn_normed, ffn_normed_out),
            copies.start(active, active_out),
            copies.start(slope, slope_out),
        ]
        saves.append(copies.start(second, second_out))
        grad[...] = nt(slope[...], w_in[...])
        norm_backward(second, gains[2], biases[2], grad, cotangent, carried, sums_out, 2)
        saves.append(copies.start(carried, carried_out))
        branch[...] = carried[...].astype(bf16)
        saves.append(copies.start(branch, branch_out))
        grad_mixed[...] = nt(branch[...], w_cross[:, D : 2 * D]).astype(bf16)
        attention_backward(
            queries, 0, kv, 0, kv, D, probs, grad_mixed, None, 0, dkv, 0, dkv, D, together=4, scores_ref=scores
        )
        saves.append(copies.start(scores, scores_out))
        saves.append(copies.start(dkv, dkv_out))
        for save in saves:
            save.wait()


def feed_kernel(
    section_ref, place_ref, dkv_in, kv_in, cotangent_in, gain_in, bias_in, sums_in, down_w, cross_w,
    memory_in, second_in, e_active_in, e_slope_in,
    query_normed_in, scores_in, mixed_in, branch_in, ffn_normed_in, d_active_in, d_slope_in,
    grad_out, sums_out, dq_out, slope_out, in_send, in_keep, down_send, down_keep, cross_send, cross_keep,
    w_down, w_cross, dkv, memory, second, active, slope, normed, branch, mixed, dq, query_normed,
    cotangent, scores, keys, grad, cross_grad, in_grad, down_grad, gains, biases, semaphores,
):
    section, place = section_ref[0], place_ref[0]
    sums_out[...] = sums_in[...]

    @pl.when(section == 0)
    def encoder():
        copies = Copies(semaphores)
        loads = [copies.start(memory_in, memory), copies.start(dkv_in, dkv)]
        load_cross = copies.start(cross_w, w_cross)
        load_cotangent = copies.start(cotangent_in, cotangent)
        load_norms = [copies.start(gain_in, gains), copies.start(bias_in, biases)]
        load_second = copies.start(second_in, second)
        load_down = copies.start(down_w, w_down)
        load_slope = copies.start(e_slope_in, slope)
        load_active = copies.start(e_active_in, active)
        load_normed = copies.start(query_normed_in, normed)
        for load in loads:
            load.wait()

        def across(i):
            put_grad(cross_grad, i, tn(memory[...], dkv[:, tile_at(i, TILE)]))

        loop(2 * D // TILE, across)
        load_cross.wait()
        load_cotangent.wait()
        grad[...] = cotangent[...].astype(f32) + nt(dkv[...], w_cross[...])
        load_second.wait()
        for load in load_norms:
            load.wait()
        norm_backward(second, gains[2], biases[2], grad, None, second, sums_out, 2)
        branch[...] = second[...].astype(bf16)
        load_down.wait()
        load_slope.wait()

        def back(i):
            columns = tile_at(i, TILE)
            slope[:, columns] = (slope[:, columns].astype(f32) * nt(branch[...], w_down[columns, :])).astype(bf16)

        loop(FF // TILE, back)
        saves = [copies.start(second, grad_out), copies.start(slope, slope_out)]
        load_active.wait()
        load_normed.wait()
        for save in saves:
            save.wait()

    @pl.when(section == 1)
    def decoder():
        copies = Copies(semaphores)
        loads = [copies.start(kv_in.at[:, pl.ds(0, D)], keys), copies.start(scores_in, scores)]
        nexts = [
            copies.start(query_normed_in, query_normed),
            copies.start(mixed_in, mixed),
            copies.start(branch_in, memory),
        ]
        others = [
            copies.start(d_active_in, active),
            copies.start(cotangent_in, branch),
            copies.start(d_slope_in, slope),
            copies.start(ffn_normed_in, normed),
        ]
        for load in loads:
            load.wait()
        query_gradient(scores, keys, dq)
        save = copies.start(dq, dq_out)
        for load in nexts:
            load.wait()
        put_grad(cross_grad, 0, tn(query_normed[...], dq[...]))
        put_grad(cross_grad, 1, tn(mixed[...], memory[...]))
        for load in others:
            load.wait()
        save.wait()

    copies = Copies(semaphores)
    saves = []

    def lower(i):
        columns = tile_at(i, TILE)
        value = tn(active[:, columns], branch[...]).astype(bf16)
        if down_grad.shape[1] == 1:
            down_grad[0, 0, 0, columns, :] = value
        else:
            wide, two, narrow, rows, width = down_grad.shape
            step = TILE // (two * narrow * rows)
            down_grad[tile_at(i, step)] = value.reshape(step, two, narrow, rows, width)

    def upper(i):
        value = tn(normed[...], slope[:, tile_at(i, TILE)])
        if cross_grad.shape[1] == 2 and i == FF // TILE - 1:
            put_grad(cross_grad, 2, value)
        else:
            put_grad(in_grad, i, value)

    for i in range(FF // TILE)[::-1]:
        upper(i)
        if i == FF // TILE - 1:
            saves += send_halves(copies, cross_grad, place, 2, cross_send, cross_keep)
    saves += send_halves(copies, in_grad, place, 0, in_send, in_keep)
    mine = lax.rem(lax.div(place, 2), 2)
    for i in range(FF // TILE):
        lower(i)
        if down_grad.shape[0] == FF // TILE:
            saves.append(copies.start(down_grad.at[i, 1 - mine], down_send.at[i]))
            saves.append(copies.start(down_grad.at[i, mine], down_keep.at[i]))
    if down_grad.shape[0] != FF // TILE:
        saves += send_halves(copies, down_grad, place, 1, down_send, down_keep)
    for save in saves:
        save.wait()


def self_kernel(
    section_ref, place_ref, grad_in, tokens_in, gain_in, bias_in, sums_in, out_w, qkv_w, cross_w, down_w, in_w, slope_in,
    qkv_in, probs_in, normed_in, mixed_in, dq_in, first_in, second_in, carried_in, active_in, memory_in,
    grad_out, sums_out, output_out, qv_send, qv_keep, k_send, k_keep, o_send, o_keep,
    w_o, w_qkv, w_query, carried, qkv, probs, mixed, dq, first, branch, grad_mixed, dqkv, grad, normed,
    tokens_ref, result, w_down, w_in, active, second, output, qv_grad, k_grad, o_grad, gains, biases, semaphores,
):
    del memory_in
    section, place = section_ref[0], place_ref[0]
    ahead = Copies(semaphores)

    @pl.when(section == 0)
    def encoder_loads():
        own = Copies(semaphores)
        own.start(slope_in, active)
        own.start(in_w, w_in)
        own.start(first_in, first)
        own.start(grad_in, carried)
        own.start(gain_in, gains)
        own.start(bias_in, biases)

    @pl.when(section == 1)
    def decoder_loads():
        own = Copies(semaphores)
        own.start(carried_in, carried)
        own.start(dq_in, dq)
        own.start(cross_w.at[:, pl.ds(0, D)], w_query)
        own.start(first_in, first)
        own.start(gain_in, gains)
        own.start(bias_in, biases)

    copies = Copies(semaphores)
    copies.count = 6
    load_o = copies.start(out_w, w_o)
    load_qkv = copies.start(qkv_in, qkv)
    load_probs = copies.start(probs_in, probs)
    load_mixed = copies.start(mixed_in, mixed)
    load_w = copies.start(qkv_w, w_qkv)
    load_tokens = copies.start(tokens_in, tokens_ref)
    load_normed = copies.start(normed_in, normed)
    sums_out[...] = sums_in[...]

    @pl.when(section == 0)
    def encoder():
        pieces = [(slope_in, active), (in_w, w_in), (first_in, first), (grad_in, carried)]
        for at, (source, target) in enumerate(pieces + [(gain_in, gains), (bias_in, biases)]):
            ahead.same(source, target, at).wait()
        grad[...] = nt(active[...], w_in[...])

    @pl.when(section == 1)
    def decoder():
        pieces = [(carried_in, carried), (dq_in, dq), (cross_w.at[:, pl.ds(0, D)], w_query), (first_in, first)]
        for at, (source, target) in enumerate(pieces + [(gain_in, gains), (bias_in, biases)]):
            ahead.same(source, target, at).wait()
        for at, (source, target) in enumerate([(active_in, active), (down_w, w_down), (second_in, second)]):
            ahead.same(source, target, at).start()
        grad[...] = nt(dq[...], w_query[...])

    norm_backward(first, gains[1], biases[1], grad, carried, carried, sums_out, 1)
    branch[...] = carried[...].astype(bf16)
    load_o.wait()
    grad_mixed[...] = nt(branch[...], w_o[...]).astype(bf16)
    load_mixed.wait()
    split = len(qv_grad.shape) == 6
    put_o = (lambda *own: put_turned(*own, True)) if split else put_grad
    put_qv = (lambda *own: put_turned(*own, False)) if split else put_grad
    put_o(o_grad, 0, tn(mixed[...], branch[...]))
    if split:
        piece = lambda far, at, other: o_grad.at[far, at, :, other]
        saves = send_rows(copies, piece, place, 2, FF // 16, o_send, o_keep)
    else:
        saves = send_halves(copies, o_grad, place, 2, o_send, o_keep)
    load_qkv.wait()
    load_probs.wait()
    attention_backward(qkv, 0, qkv, D, qkv, 2 * D, probs, grad_mixed, dqkv, 0, dqkv, D, dqkv, 2 * D, together=4)
    load_w.wait()
    grad[...] = nt(dqkv[...], w_qkv[...])
    load_tokens.wait()
    norm_backward(tokens_ref, gains[0], biases[0], grad, carried, result, sums_out, 0)
    saves.append(copies.start(result, grad_out))
    load_normed.wait()
    turned = normed[...].T
    put_qv(qv_grad, 0, nn(turned, dqkv[:, 0:D]))
    put_qv(qv_grad, 1, nn(turned, dqkv[:, 2 * D : 3 * D]))
    if split:
        piece = lambda far, at, other: qv_grad.at[far, at, :, other]
        saves += send_rows(copies, piece, place, 0, 3 * D // 16, qv_send, qv_keep)
    else:
        saves += send_halves(copies, qv_grad, place, 0, qv_send, qv_keep)
    put_grad(k_grad, 0, nn(turned, dqkv[:, D : 2 * D]))
    if split:
        piece = lambda far, at, other: k_grad.at[pl.ds(2 * far, 2), at, other]
        saves += send_rows(copies, piece, place, 1, 3 * D // 16, k_send, k_keep)
    else:
        saves += send_halves(copies, k_grad, place, 1, k_send, k_keep)

    @pl.when(section == 1)
    def decoder_output():
        for at, (source, target) in enumerate([(active_in, active), (down_w, w_down), (second_in, second)]):
            ahead.same(source, target, at).wait()
        output[...] = (second[...] + nn(active[...], w_down[...])).astype(bf16)
        save = ahead.same(output, output_out, 0)
        save.start()
        save.wait()

    for save in saves:
        save.wait()


SMEM = pl.BlockSpec(memory_space=pltpu.SMEM)
VMEM = pl.BlockSpec(memory_space=pltpu.VMEM)
ANY = pl.BlockSpec(memory_space=pl.ANY)
HBM = pl.BlockSpec(memory_space=pltpu.HBM)


def call(kernel, operands, outs, scratch, copies, flops, aliases=None, name=None, limit=VMEM_LIMIT >> 20):
    shapes = [jax.ShapeDtypeStruct(shape, dtype) for spec, shape, dtype in outs]
    moved = sum(array.size * array.dtype.itemsize for spec, array in operands)
    moved += sum(shape.size * shape.dtype.itemsize for shape in shapes)
    return pl.pallas_call(
        kernel,
        out_shape=shapes,
        in_specs=[spec for spec, array in operands],
        out_specs=[spec for spec, shape, dtype in outs],
        scratch_shapes=[pltpu.VMEM(shape, dtype) for shape, dtype in scratch] + [pltpu.SemaphoreType.DMA((copies,))],
        input_output_aliases=aliases or {},
        compiler_params=pltpu.CompilerParams(vmem_limit_bytes=limit << 20),
        cost_estimate=pl.CostEstimate(flops=int(flops), bytes_accessed=moved, transcendentals=0),
        name=name,
    )(*[array for spec, array in operands])


def split_shape(size, bit, whole):
    return (size // 2 ** (bit + 1), 2, 2**bit) if whole else (1, 1, 1)


def across(value, bit):
    return lax.ppermute(value, "batch", [(i, i ^ (2**bit)) for i in range(lax.axis_size("batch"))])


def halves(value, axis, bit):
    mine = lax.rem(lax.axis_index("batch") // (2**bit), 2)
    pick = lambda at: lax.dynamic_index_in_dim(value, at, axis, keepdims=False)
    return pick(1 - mine), pick(mine)


def total(kept, came):
    return kept.astype(f32) + came.reshape(kept.shape).astype(f32)


def joined(early, late):
    return lax.dynamic_update_slice(late, early.transpose(1, 0, 2, 3), (0, 0, 0, 0))


def flat(value):
    return value.reshape(-1, TILE)


def chained(early, late, sums):
    (in_keep, in_came), (down_keep, down_came), (cross_keep, cross_came) = early
    (qv_send, qv_keep), (k_send, k_keep), (o_send, o_keep) = late
    turn = lax.optimization_barrier

    def send_first(kept, came, axis, bit):
        kept_halves, came_halves = halves(kept, axis, bit), halves(came.reshape(kept.shape), axis, bit)
        return total(kept_halves[0], came_halves[0]).astype(bf16), (kept_halves[1], came_halves[1])

    def stays(rest):
        return total(*rest).astype(bf16)

    cube = lambda value: value.reshape(2, 2, 2, -1, TILE)
    c_send, c_rest = send_first(cube(cross_keep), cross_came, 2, 0)
    c_send, in_keep = turn((joined(c_send, qv_send), in_keep))
    c_came = across(c_send, 0)
    a_send, a_rest = send_first(cube(in_keep), in_came, 2, 1)
    a_send, down_keep = turn((joined(a_send, k_send), down_keep))
    a_came = across(a_send, 1)
    b_send, b_rest = send_first(cube(down_keep), down_came, 1, 2)
    b_send, a_rest, b_rest, c_rest, sums = turn((joined(b_send, o_send), a_rest, b_rest, c_rest, sums))
    b_came = across(b_send, 2)
    y_sums = across(sums, 1)
    a_keep, b_keep, c_keep = joined(stays(a_rest), k_keep), joined(stays(b_rest), o_keep), joined(stays(c_rest), qv_keep)
    a_keep, b_keep, c_keep = turn((a_keep, b_keep, c_keep))

    c_send, c_rest = send_first(c_keep, c_came, 0, 1)
    a_send, a_rest = send_first(a_keep, a_came, 0, 2)
    b_send, b_rest = send_first(b_keep, b_came, 0, 0)
    sums = sums + y_sums
    a_send = jnp.concatenate([flat(a_send), sums.astype(bf16)], axis=0)
    a_send, b_send, c_send, a_rest, b_rest, c_rest = turn((a_send, b_send, c_send, a_rest, b_rest, c_rest))
    a_came, b_came, c_came = across(a_send, 2), across(b_send, 0), across(c_send, 1)
    a_keep, b_keep, c_keep = turn((stays(a_rest), stays(b_rest), stays(c_rest)))
    a_rows, norm_rows = a_keep.size // TILE, sums.shape[0]
    sums = sums + a_came[a_rows:].astype(f32)
    rows, down_rows, short = in_keep.shape[-2], down_keep.shape[-2], cross_keep.shape[-2]

    def third_halves(kept, came, split, bit):
        value = total(kept, came).astype(bf16)
        return halves(value[:, :split], 0, 3), halves(value[:, split:].reshape(2, 2, -1, TILE), 1, bit)

    cross_end, (qv_send, qv_keep) = third_halves(c_keep, c_came, short, 2)
    down_end, (o_send, o_keep) = third_halves(b_keep, b_came, down_rows, 1)
    in_end, (k_send, k_keep) = third_halves(a_keep, a_came[:a_rows], rows, 0)
    far_send = jnp.concatenate([in_end[0], down_end[0], cross_end[0]], axis=0)
    far_came = across(far_send, 3)
    k_send = jnp.concatenate([flat(k_send), sums.astype(bf16)], axis=0)
    o_send, k_send, qv_send = turn((o_send, k_send, qv_send))
    o_came, k_came, qv_came = across(o_send, 1), across(k_send, 0), across(qv_send, 2)
    k_rows = k_keep.size // TILE
    sums = sums + k_came[k_rows:].astype(f32)
    k_came = k_came[:k_rows]

    late = ((qv_keep, qv_came), (k_keep, k_came), (o_keep, o_came))
    ends = [halves(total(kept, came).astype(bf16), 0, 3) for kept, came in late]
    padded = jnp.concatenate([sums, jnp.zeros_like(sums)], axis=0).astype(bf16)
    last_send = jnp.concatenate([end[0] for end in ends] + [padded], axis=0)
    last_send, far_came = turn((last_send, far_came))
    last_came = across(last_send, 3)
    in_sum = total(in_end[1], far_came[:rows])
    down_sum = total(down_end[1], far_came[rows : rows + down_rows])
    cross_sum = total(cross_end[1], far_came[rows + down_rows :])
    return [end[1] for end in ends], last_came, sums, in_sum, down_sum, cross_sum


class Part:
    def __init__(self, send, keep, order, size, row_major=False):
        count = size.bit_length() - 1
        self.order = list(order)
        self.rides = None
        self.axes = list(range(count))[::-1]
        self.send = None
        if len(send.shape) == 5:
            value = by_destination(send.reshape(send.shape[-2:]), size, row_major)
            self.value = value.reshape((2,) * count + value.shape[1:])
        else:
            self.axes.remove(order[0])
            self.send = send
            self.value = keep.reshape((2,) * (count - 1) + keep.shape[-2:])


def exchange(parts):
    size = lax.axis_size("batch")
    place = lax.axis_index("batch")
    parts = [part for part in parts if part.order]
    by_bit = {}
    for part in parts:
        by_bit.setdefault(part.order[0], []).append(part)
    for bit, group in by_bit.items():
        mine = lax.rem(place // (2**bit), 2)
        sends = []
        for part in group:
            send = part.send
            if send is None:
                at = part.axes.index(bit)
                send = lax.dynamic_index_in_dim(part.value, 1 - mine, at, keepdims=False)
                part.value = lax.dynamic_index_in_dim(part.value, mine, at, keepdims=False)
                part.axes.remove(bit)
            part.send = None
            part.order = part.order[1:]
            sends.append(send.reshape(-1, TILE))
            if part.rides is not None:
                sends.append(part.rides.astype(bf16))
        payload = sends[0] if len(sends) == 1 else jnp.concatenate(sends, axis=0)
        came = lax.ppermute(payload, "batch", [(i, i ^ (2**bit)) for i in range(size)])
        start = 0
        for part in group:
            rows = part.value.size // TILE
            total = part.value.astype(f32) + came[start : start + rows].reshape(part.value.shape).astype(f32)
            part.value = total.astype(bf16) if part.order else total
            start += rows
            if part.rides is not None:
                part.rides = part.rides + came[start : start + part.rides.shape[0]].astype(f32)
                start += part.rides.shape[0]


def fence(parts):
    held = lax.optimization_barrier([(part.value, part.send, part.rides) for part in parts])
    for part, (value, send, rides) in zip(parts, held):
        part.value, part.send, part.rides = value, send, rides


def by_destination(value, size, row_major):
    if row_major:
        return value.reshape(size, -1, TILE)
    return value.reshape(-1, size, D // size, TILE).transpose(1, 0, 2, 3).reshape(size, -1, TILE)


def columns_of(total):
    rows = D // lax.axis_size("batch")
    return total.reshape(-1, rows, TILE).transpose(1, 0, 2).reshape(rows, -1)


def body(
    inputs,
    cotangent,
    lengths,
    norm_gain,
    norm_bias,
    attn_qkv,
    attn_out,
    ffn_in,
    ffn_out,
    cross_proj,
):
    section = lax.axis_index("section").astype(jnp.int32).reshape(1)
    place = lax.axis_index("batch").astype(jnp.int32).reshape(1)
    size = lax.axis_size("batch")
    count = size.bit_length() - 1
    whole = size == 16

    in_rows, cross_rows = (3 * D, 3 * D) if whole else (FF, 2 * D)

    def grad_scratch(bit, rows):
        lead = split_shape(size, bit, whole)
        return (lead + (rows // math.prod(lead), TILE), bf16)

    def grad_outs(bit, rows):
        if not whole:
            return [(HBM, (1, 1, 1, rows, TILE), bf16), (HBM, (16, TILE), bf16)]
        wide, two, narrow = split_shape(size, bit, whole)
        return [(HBM, (wide, narrow, rows // size, TILE), bf16)] * 2

    rows = inputs.shape[1]
    T = rows * SEQ
    tokens = inputs[0].reshape(T, D)
    cot = cotangent[0].reshape(T, D)
    gain, bias = norm_gain.transpose(1, 0, 2), norm_bias.transpose(1, 0, 2)
    w_qkv, w_o, w_in, w_down, w_cross = attn_qkv[0], attn_out[0], ffn_in[0], ffn_out[0], cross_proj[0]
    unit = 2.0 * T * D * D
    norm_scratch = [((3, 1, D), f32), ((3, 1, D), f32)]

    memory, kv, qkv, probs, mixed, first, active, slope, second, query_normed, queries, normed = call(
        forward_kernel,
        [(SMEM, section), (SMEM, lengths), (HBM, tokens), (HBM, gain), (HBM, bias)]
        + [(HBM, w) for w in (w_qkv, w_o, w_in, w_down, w_cross)],
        [(HBM, (T, D), bf16), (HBM, (T, 2 * D), bf16), (HBM, (T, 3 * D), bf16)]
        + [(HBM, (rows * HEADS, SEQ, SEQ), bf16), (HBM, (T, D), bf16), (HBM, (T, D), f32)]
        + [(HBM, (T, FF), bf16), (HBM, (T, FF), bf16), (HBM, (T, D), f32)]
        + [(HBM, (T, D), bf16)] * 3,
        [((D, 3 * D), bf16), ((D, D), bf16), ((D, FF), bf16), ((FF, D), bf16), ((D, 2 * D), bf16)]
        + [((T, D), bf16), ((T, 3 * D), bf16), ((rows * HEADS, SEQ, SEQ), bf16), ((T, D), bf16), ((T, D), f32)]
        + [((T, FF), bf16), ((T, FF), bf16), ((T, D), f32), ((T, 2 * D), bf16), ((rows, SEQ, SEQ), f32)]
        + [((T, D), bf16)] * 3
        + norm_scratch,
        20,
        24 * unit,
        name="forward",
    )
    kv_came = lax.ppermute(kv, "section", [(0, 1)])
    middle = call(
        middle_kernel,
        [(SMEM, section), (SMEM, lengths), (ANY, kv_came), (HBM, first), (HBM, queries), (HBM, cot), (HBM, gain), (HBM, bias)]
        + [(HBM, w) for w in (w_in, w_down, w_cross)],
        [(HBM, (T, 2 * D), bf16), (VMEM, (8, D), f32), (HBM, (rows * HEADS, SEQ, SEQ), bf16)]
        + [(HBM, (T, D), bf16)] * 3
        + [(HBM, (T, FF), bf16), (HBM, (T, FF), bf16), (HBM, (T, D), f32), (HBM, (T, D), f32)],
        [((D, FF), bf16), ((FF, D), bf16), ((D, 2 * D), bf16), ((T, 2 * D), bf16), ((T, D), f32), ((T, D), bf16)]
        + [((T, D), bf16), ((rows * HEADS, SEQ, SEQ), bf16), ((T, D), bf16), ((T, D), f32)]
        + [((T, D), bf16), ((T, FF), bf16), ((T, FF), bf16), ((T, D), f32), ((T, D), bf16), ((T, D), bf16)]
        + [((rows * HEADS, SEQ, SEQ), bf16), ((T, 2 * D), bf16), ((rows, SEQ, SEQ), f32), ((T, D), f32)]
        + norm_scratch,
        20,
        40 * unit,
        name="middle",
    )
    dkv, sums, scores, cross_mixed, branch, ffn_normed, d_active, d_slope, d_second, d_carried = middle
    dkv_came = lax.ppermute(dkv, "section", [(1, 0)])
    grad_first, sums, dq, e_slope, *early = call(
        feed_kernel,
        [(SMEM, section), (SMEM, place), (ANY, dkv_came), (ANY, kv_came), (HBM, cot), (HBM, gain), (HBM, bias), (VMEM, sums)]
        + [(HBM, w) for w in (w_down, w_cross)]
        + [(HBM, a) for a in (memory, second, active, slope)]
        + [(HBM, a) for a in (query_normed, scores, cross_mixed, branch, ffn_normed, d_active, d_slope)],
        [(HBM, (T, D), f32), (VMEM, (8, D), f32), (HBM, (T, D), bf16), (HBM, (T, FF), bf16)]
        + grad_outs(0, in_rows) + grad_outs(1, FF) + grad_outs(2, cross_rows),
        [((FF, D), bf16), ((D, 2 * D), bf16), ((T, 2 * D), bf16), ((T, D), bf16), ((T, D), f32)]
        + [((T, FF), bf16), ((T, FF), bf16), ((T, D), bf16), ((T, D), bf16), ((T, D), bf16)]
        + [((T, D), bf16), ((T, D), bf16), ((T, D), bf16), ((rows * HEADS, SEQ, SEQ), bf16), ((T, D), bf16)]
        + [((T, D), f32)]
        + [grad_scratch(2, cross_rows), grad_scratch(0, in_rows), grad_scratch(1, FF)]
        + norm_scratch,
        24,
        24 * unit,
        name="feed",
    )
    if whole:
        early_came = [across(early[0], 0), across(early[2], 1), across(early[4], 2)]
    else:
        last = list(range(3, count))
        early = [
            Part(early[0], early[1], [0, 2, 1] + last, size),
            Part(early[2], early[3], [1, 0, 2] + last, size, True),
            Part(early[4], early[5], [2, 1, 0] + last, size),
        ]
        exchange(early)
    qv_scratch, qv_outs = grad_scratch(0, 2 * D), grad_outs(0, 2 * D)
    k_outs = grad_outs(1, D)
    o_scratch, o_outs = grad_scratch(2, D), grad_outs(2, D)
    if whole:
        per_block = lambda elements: elements // size
        qv_scratch = ((2, 2, 2, 2, per_block(2 * D), TILE), bf16)
        qv_outs = [(HBM, (2, 2, per_block(cross_rows + 4 * D), TILE), bf16)] * 2
        k_outs = [(HBM, (2, 2, per_block(in_rows + 2 * D), TILE), bf16)] * 2
        o_scratch = ((2, 2, 2, 2, per_block(D), TILE), bf16)
        o_outs = [(HBM, (2, 2, per_block(FF + 2 * D), TILE), bf16)] * 2
    input_grad, sums, output, *late = call(
        self_kernel,
        [(SMEM, section), (SMEM, place), (HBM, grad_first), (HBM, tokens), (HBM, gain), (HBM, bias), (VMEM, sums)]
        + [(HBM, a) for a in (w_o, w_qkv, w_cross, w_down, w_in, e_slope, qkv, probs, normed, mixed, dq, first)]
        + [(HBM, a) for a in (d_second, d_carried, d_active, memory)],
        [(HBM, (T, D), f32), (VMEM, (8, D), f32), (HBM, (T, D), bf16)] + qv_outs + k_outs + o_outs,
        [((D, D), bf16), ((D, 3 * D), bf16), ((D, D), bf16), ((T, D), f32), ((T, 3 * D), bf16)]
        + [((rows * HEADS, SEQ, SEQ), bf16), ((T, D), bf16), ((T, D), bf16), ((T, D), f32)]
        + [((T, D), bf16), ((T, D), bf16), ((T, 3 * D), bf16), ((T, D), f32), ((T, D), bf16)]
        + [((T, D), bf16), ((T, D), f32), ((FF, D), bf16), ((D, FF), bf16), ((T, FF), bf16)]
        + [((T, D), f32), ((T, D), bf16), qv_scratch, grad_scratch(1, D), o_scratch]
        + norm_scratch,
        44,
        16 * unit,
        aliases={22: 2},
        name="self_back",
    )
    width = D // size
    if whole:
        early = [(early[1], early_came[0]), (early[3], early_came[1]), (early[5], early_came[2])]
        late = [(late[0], late[1]), (late[2], late[3]), (late[4], late[5])]
        kept, came, sums, in_sum, down_sum, cross_sum = chained(early, late, sums)
        qkv_sum, o_sum, gain_sum, bias_sum = call(
            end_kernel,
            [(VMEM, a) for a in (*kept, came, sums)] + [(SMEM, place)],
            [(HBM, (width, 3 * D), f32), (HBM, (width, D), f32), (HBM, (3, 1, width), f32), (HBM, (3, 1, width), f32)],
            [((width, 3 * D), f32), ((width, D), f32), ((3, 1, width), f32), ((3, 1, width), f32)],
            4,
            1.0,
            name="ends",
            limit=8,
        )
        in_sum, cross_sum = jnp.concatenate([in_sum, cross_sum[2 * width :]], axis=0), cross_sum[: 2 * width]
    else:
        late = [
            Part(late[0], late[1], [0, 1, 2] + last, size),
            Part(late[2], late[3], [1, 2, 0] + last, size),
            Part(late[4], late[5], [2, 0, 1] + last, size),
        ]
        late[1].rides = sums
        for step in range(count):
            fence(early + late)
            exchange(early + late)
        sums = late[1].rides
        totals = [part.value.reshape(-1, TILE) for part in early + late]
        in_sum, down_sum, cross_sum, qv_sum, k_sum, o_sum = totals
        qkv_sum = jnp.concatenate([qv_sum[:width], k_sum, qv_sum[width:]], axis=1)
        norm_grads = lax.dynamic_slice_in_dim(sums, lax.axis_index("batch") * width, width, axis=1)
        gain_sum, bias_sum = norm_grads[0:3].reshape(3, 1, width), norm_grads[3:6].reshape(3, 1, width)
    return (
        output.reshape(1, rows, SEQ, D),
        input_grad.reshape(1, rows, SEQ, D),
        gain_sum.transpose(1, 0, 2),
        bias_sum.transpose(1, 0, 2),
        qkv_sum[None],
        o_sum[None],
        columns_of(in_sum)[None],
        down_sum[None],
        columns_of(cross_sum)[None],
    )


def solution(mesh):
    placed = (
        P("section", "batch", None, None),
        P("section", "batch", None, None),
        P("batch", None, None),
        P("section", None, None),
        P("section", None, None),
        P("section", None, None),
        P("section", None, None),
        P("section", None, None),
        P("section", None, None),
        P("section", None, None),
    )
    return jax.shard_map(
        body,
        mesh=mesh,
        in_specs=placed,
        out_specs=(
            P("section", "batch", None, None),
            P("section", "batch", None, None),
            P("section", None, "batch"),
            P("section", None, "batch"),
            P("section", "batch", None),
            P("section", "batch", None),
            P("section", "batch", None),
            P("section", "batch", None),
            P("section", "batch", None),
        ),
        check_vma=False,
    )
```
